32 devices in a mesh: seq: 8 (over y, x, core), head: 4 (over z).
Axes of the slice: x: 2, y: 2, z: 4, core: 2. Of those that a mesh axis runs over, the one named last changes fastest.
Arguments:
- queries: bfloat16 [16384, 2048], P('seq', 'head'), may hold values from -4.5 to 4.5
- key_vectors: bfloat16 [16384, 2048], P('seq', 'head'), may hold values from -4.5 to 4.5
- value_vectors: bfloat16 [16384, 2048], P('seq', 'head'), may hold values from -18 to 18
- w_out: bfloat16 [2048, 2048], P('seq'), may hold values from -0.125 to 0.125
Outputs:
- projected: bfloat16 [16384, 2048], P(('seq', 'head'))
The draws below stay inside these ranges and needn't reach their ends.
All inputs are finite; a program needn't handle non-finite values.
Results may differ from the reference program's by a relative error of at most 0.0053.
Values may be sent and summed in bfloat16 or wider, within the bound.
A program may use at most 128 MiB of HBM per device.

```python
import math
import jax
import jax.numpy as jnp
from jax import lax

H = 16
HD = 128
W = 1024
D = 2048
TOKENS = 16384


def draw_queries(key, part):
    base_key = jax.random.fold_in(key, 1)
    base_draw = jax.random.truncated_normal(base_key, -4.5, 4.5, (TOKENS, D), jnp.float32)
    return base_draw.astype(jnp.bfloat16)


def draw_key_vectors(key, part):
    base_key = jax.random.fold_in(key, 2)
    base_draw = jax.random.truncated_normal(base_key, -4.5, 4.5, (TOKENS, D), jnp.float32)
    return base_draw.astype(jnp.bfloat16)


def draw_value_vectors(key, part):
    row_scale = jnp.exp(jax.random.uniform(jax.random.fold_in(key, 1), (TOKENS, 1), jnp.float32, math.log(0.3), math.log(3.0)))
    col_scale = jnp.exp(jax.random.uniform(jax.random.fold_in(key, 2), (1, D), jnp.float32, math.log(0.5), math.log(2.0)))
    noise_draw = jax.random.truncated_normal(jax.random.fold_in(key, 4), -3.0, 3.0, (TOKENS, D), jnp.float32)
    drawn = row_scale * col_scale * noise_draw
    return drawn.astype(jnp.bfloat16)


def shard_levels(own_key, extent, pieces, least, largest):
    def one(dim, shards_of):
        draws = jax.random.uniform(jax.random.fold_in(jax.random.fold_in(own_key, 6), dim), (shards_of,), jnp.float32, least / len(pieces), largest / len(pieces))
        return jnp.repeat(jnp.exp(draws), extent[dim] // shards_of).reshape((-1,) + (1,) * (len(extent) - dim - 1))

    factor_of = one(*pieces[0])
    for cut in pieces[1:]:
        factor_of = factor_of * one(*cut)
    return factor_of


def normal_values(rng, shape, width, bound, cuts=(), kind=jnp.bfloat16):
    factor_of = shard_levels(rng, shape, cuts, -0.22, 0.18) if cuts else 1.0
    array = jax.random.normal(rng, shape, jnp.float32) * width * factor_of
    return jnp.minimum(jnp.maximum(array, -bound), bound).astype(kind)


def setup_inputs(seed: int = 0) -> dict:
    key_of = jax.random.split(jax.random.key(seed), 5)
    return {
        "queries": draw_queries(jax.random.fold_in(key_of[4], 71), 0),
        "key_vectors": draw_key_vectors(jax.random.fold_in(key_of[4], 71), 0),
        "value_vectors": draw_value_vectors(jax.random.fold_in(key_of[4], 71), 0),
        "w_out": normal_values(key_of[3], (D, D), D ** -0.5, 0.125, ((0, 8),)),
    }


norm_eps = 1e-06

def normalize(branch):
    return branch * lax.rsqrt(lax.optimization_barrier(jnp.mean(branch * branch, axis=-1, keepdims=True)) + norm_eps)

def window_head(query_head, key_head, value_head):
    block_rows = math.gcd(TOKENS, 256)
    key_span = block_rows + W
    score_scale = 1.0 / math.sqrt(HD)
    window_keys = jnp.concatenate([jnp.zeros((W, HD), jnp.bfloat16), key_head], axis=0)
    window_values = jnp.concatenate([jnp.zeros((W, HD), jnp.bfloat16), value_head], axis=0)

    def one_block(block_start):
        query_block = lax.dynamic_slice_in_dim(query_head, block_start, block_rows, 0)
        key_block = lax.dynamic_slice_in_dim(window_keys, block_start, key_span, 0)
        value_block = lax.dynamic_slice_in_dim(window_values, block_start, key_span, 0)
        scores = jnp.dot(query_block, key_block.T, preferred_element_type=jnp.float32) * score_scale
        row_index = block_start + jnp.arange(block_rows, dtype=jnp.int32)[:, None]
        col_index = block_start + jnp.arange(key_span, dtype=jnp.int32)[None, :]
        allowed = (col_index > row_index) & (col_index <= row_index + W) & (col_index >= W)
        scores = jnp.where(allowed, scores, -jnp.inf)
        row_top = lax.optimization_barrier(jnp.max(scores, axis=-1, keepdims=True))
        weights = jnp.where(allowed, jnp.exp(scores - row_top), 0.0).astype(jnp.bfloat16)
        return jnp.dot(weights, value_block, preferred_element_type=jnp.float32)
    starts = jnp.arange(TOKENS // block_rows, dtype=jnp.int32) * block_rows
    return lax.map(one_block, starts).reshape(TOKENS, HD)

def linear_head(query_head, key_head, value_head):
    block_rows = math.gcd(TOKENS, 512)
    block_count = TOKENS // block_rows
    exact_output = lax.Precision.HIGHEST
    blocked_queries = query_head.reshape(block_count, block_rows, HD).astype(jnp.float32)
    blocked_keys = key_head.reshape(block_count, block_rows, HD).astype(jnp.float32)
    blocked_values = value_head.reshape(block_count, block_rows, HD).astype(jnp.float32)
    intra_block_scores = jnp.einsum('upn,uwn->upw', blocked_queries, blocked_keys, precision=exact_output)
    causal = jnp.arange(block_rows, dtype=jnp.int32)[:, None] >= jnp.arange(block_rows, dtype=jnp.int32)[None, :]
    intra_block_scores = jnp.where(causal[None], intra_block_scores, 0.0)
    local_block_terms = jnp.einsum('vyc,vca->vya', intra_block_scores, blocked_values, precision=exact_output)
    state_increments = jnp.einsum('tsp,tsw->tpw', blocked_keys, blocked_values, precision=exact_output)
    running = jnp.cumsum(state_increments, axis=0)
    preceding_state = jnp.concatenate([jnp.zeros_like(state_increments[:1]), running[:-1]], axis=0)
    carried_state_sum = jnp.einsum('viu,vuh->vih', blocked_queries, preceding_state, precision=exact_output)
    return (local_block_terms + carried_state_sum).reshape(TOKENS, HD)

def reference(queries, key_vectors, value_vectors, w_out):
    head_shape = (TOKENS, H, HD)
    query_heads = jnp.transpose(queries.reshape(head_shape), (1, 0, 2))
    key_heads = jnp.transpose(key_vectors.reshape(head_shape), (1, 0, 2))
    value_heads = jnp.transpose(value_vectors.reshape(head_shape), (1, 0, 2))

    def per_head(triple):
        query_head, key_head, value_head = triple
        soft_head = window_head(query_head, key_head, value_head)
        linear = linear_head(query_head, key_head, value_head)
        return (0.5 * (normalize(soft_head) + normalize(linear))).astype(jnp.bfloat16)
    mixed_heads = lax.map(per_head, (query_heads, key_heads, value_heads))
    attended = jnp.transpose(mixed_heads, (1, 0, 2)).reshape(TOKENS, D)
    return jnp.dot(attended, w_out, preferred_element_type=jnp.float32).astype(jnp.bfloat16)
```

```python
import functools
import math

import jax
import jax.numpy as jnp
from jax import lax
from jax.experimental import pallas as pl
from jax.experimental.pallas import tpu as pltpu
from jax.sharding import PartitionSpec as P

HD = 128
W = 1024
NORM_EPS = 1e-06
F32 = jnp.float32
BF16 = jnp.bfloat16


def dot_nt(a, b):
    return lax.dot_general(a, b, (((1,), (1,)), ((), ())), preferred_element_type=F32)


def dot_tn(a, b):
    return lax.dot_general(a, b, (((0,), (0,)), ((), ())), preferred_element_type=F32)


def dot_nn(a, b):
    return jnp.dot(a, b, preferred_element_type=F32)


def normalize(branch):
    return branch * lax.rsqrt(jnp.mean(branch * branch, axis=-1, keepdims=True) + NORM_EPS)


def hi_lo(values):
    upper = values.astype(BF16)
    lower = (values - upper.astype(F32)).astype(BF16)
    return upper, lower


def totals_kernel(k_ref, v_ref, out_ref):
    for h in range(out_ref.shape[0]):
        cols = slice(h * HD, (h + 1) * HD)
        out_ref[h] = dot_tn(k_ref[:, cols], v_ref[:, cols])


def attend_block(q_ref, kbuf, vbuf, states, prior_ref, b, block, h, rows):
    cols = slice(h * HD, (h + 1) * HD)
    score_scale = math.log2(math.e) / math.sqrt(HD)
    q = q_ref[pl.ds(b, rows), cols]
    s = dot_nt(q, kbuf[pl.ds(b, W + rows), cols])
    row = lax.broadcasted_iota(jnp.int32, (rows, rows), 0)
    col = lax.broadcasted_iota(jnp.int32, (rows, rows), 1)
    raw = s[:, W:]
    first = jnp.where(col > row, s[:, :rows], -jnp.inf)
    last = jnp.where(col <= row, raw, -jnp.inf)
    s = jnp.concatenate([first, s[:, rows:W], last], axis=1)
    top = jnp.max(s, axis=-1, keepdims=True)
    p = jnp.exp2((s - top) * score_scale).astype(BF16)
    soft = dot_nn(p, vbuf[pl.ds(b, W + rows), cols])

    v_own = vbuf[pl.ds(b + W, rows), cols]
    upper, lower = hi_lo(jnp.where(col <= row, raw, 0.0))
    lin = dot_nn(upper, v_own) + dot_nn(lower, v_own)
    s_upper, s_lower = hi_lo(states[block, h] + prior_ref[h])
    lin += dot_nn(jnp.concatenate([q, q], axis=1), jnp.concatenate([s_upper, s_lower], axis=0))
    return (0.5 * (normalize(soft) + normalize(lin))).astype(BF16)


def attend_kernel(rows, q_ref, k_hbm, v_hbm, rim_hbm, prior_ref, out_ref, kbuf, vbuf, states, sems):
    tok_rows, width = q_ref.shape
    heads_here = width // HD
    blocks = tok_rows // rows
    copies = [
        pltpu.make_async_copy(k_hbm, kbuf.at[pl.ds(W, tok_rows)], sems.at[0]),
        pltpu.make_async_copy(v_hbm, vbuf.at[pl.ds(W, tok_rows)], sems.at[1]),
        pltpu.make_async_copy(rim_hbm.at[0], kbuf.at[pl.ds(0, W)], sems.at[2]),
        pltpu.make_async_copy(rim_hbm.at[1], vbuf.at[pl.ds(0, W)], sems.at[3]),
    ]
    for c in copies:
        c.start()
    for c in copies:
        c.wait()

    @pl.when(lax.axis_index("seq") == 0)
    def _():
        kbuf[0:W] = jnp.broadcast_to(kbuf[W : W + 1], (W, width))
        vbuf[0:W] = jnp.zeros((W, width), BF16)

    for h in range(heads_here):
        cols = slice(h * HD, (h + 1) * HD)
        total = jnp.zeros((HD, HD), F32)
        for block in range(blocks):
            states[block, h] = total
            span = slice(W + block * rows, W + (block + 1) * rows)
            if block < blocks - 1:
                total += dot_tn(kbuf[span, cols], vbuf[span, cols])

    def one_block(block, carry):
        b = pl.multiple_of(block * rows, rows)
        for h in range(heads_here):
            out_ref[pl.ds(b, rows), h * HD : (h + 1) * HD] = attend_block(
                q_ref, kbuf, vbuf, states, prior_ref, b, block, h, rows
            )
        return carry

    lax.fori_loop(0, blocks, one_block, 0)


def earlier_total(total, axis):
    count = lax.axis_size(axis)
    me = lax.axis_index(axis)
    prior = jnp.zeros_like(total)
    bit = 1
    while bit < count:
        other = lax.ppermute(total, axis, [(i, i ^ bit) for i in range(count)])
        prior = prior + jnp.where((me & bit) != 0, other, 0.0)
        total = total + other
        bit *= 2
    return prior


def on_device(queries, key_vectors, value_vectors, w_out):
    tok_rows, width = queries.shape
    heads_here = width // HD
    count = lax.axis_size("seq")
    rows = min(256, tok_rows // lax.axis_size("head"))
    vmem = pl.BlockSpec(memory_space=pltpu.VMEM)
    hbm = pl.BlockSpec(memory_space=pl.ANY)
    total = pl.pallas_call(
        totals_kernel,
        out_shape=jax.ShapeDtypeStruct((heads_here, HD, HD), F32),
        in_specs=[vmem, vmem],
        out_specs=vmem,
        compiler_params=pltpu.CompilerParams(vmem_limit_bytes=32 << 20),
    )(key_vectors, value_vectors)
    rim = jnp.stack([key_vectors[tok_rows - W :], value_vectors[tok_rows - W :]])
    rim = lax.ppermute(rim, "seq", [(i, i + 1) for i in range(count - 1)])
    prior = earlier_total(total, "seq")
    mixed = pl.pallas_call(
        functools.partial(attend_kernel, rows),
        out_shape=jax.ShapeDtypeStruct((tok_rows, width), BF16),
        in_specs=[vmem, hbm, hbm, hbm, vmem],
        out_specs=vmem,
        scratch_shapes=[
            pltpu.VMEM((W + tok_rows, width), BF16),
            pltpu.VMEM((W + tok_rows, width), BF16),
            pltpu.VMEM((tok_rows // rows, heads_here, HD, HD), F32),
            pltpu.SemaphoreType.DMA((4,)),
        ],
        compiler_params=pltpu.CompilerParams(vmem_limit_bytes=48 << 20),
        cost_estimate=pl.CostEstimate(
            flops=2 * 2 * tok_rows * 1400 * width, bytes_accessed=8 << 20, transcendentals=0
        ),
    )(queries, key_vectors, value_vectors, rim, prior)
    regrouped = lax.all_to_all(mixed, "head", split_axis=0, concat_axis=1, tiled=True)
    projected = jnp.dot(
        regrouped,
        lax.all_gather(w_out, "seq", axis=0, tiled=True),
        preferred_element_type=F32,
    )
    return projected.astype(BF16)


def solution(mesh):
    placed = (P("seq", "head"), P("seq", "head"), P("seq", "head"), P("seq", None))
    return jax.shard_map(
        on_device, mesh=mesh, in_specs=placed, out_specs=P(("seq", "head"), None), check_vma=False
    )
```

```python
import functools
import math

import jax
import jax.numpy as jnp
from jax import lax
from jax.experimental import pallas as pl
from jax.experimental.pallas import tpu as pltpu
from jax.sharding import PartitionSpec as P

HD = 128
W = 1024
NORM_EPS = 1e-06
F32 = jnp.float32
BF16 = jnp.bfloat16
MESH = pl.DeviceIdType.MESH


def dot_nt(a, b):
    return lax.dot_general(a, b, (((1,), (1,)), ((), ())), preferred_element_type=F32)


def dot_tn(a, b):
    return lax.dot_general(a, b, (((0,), (0,)), ((), ())), preferred_element_type=F32)


def dot_nn(a, b):
    return jnp.dot(a, b, preferred_element_type=F32)


def normalize(branch):
    return branch * lax.rsqrt(jnp.mean(branch * branch, axis=-1, keepdims=True) + NORM_EPS)


def hi_lo(values):
    upper = values.astype(BF16)
    lower = (values - upper.astype(F32)).astype(BF16)
    return upper, lower


def flip(index, bit):
    return index + bit - 2 * bit * lax.rem(lax.div(index, bit), 2)


def raw_block(q_ref, kbuf, vbuf, b, h, rows):
    cols = slice(h * HD, (h + 1) * HD)
    score_scale = math.log2(math.e) / math.sqrt(HD)
    q = q_ref[pl.ds(b, rows), cols]
    s = dot_nt(q, kbuf[pl.ds(b, W + rows), cols])
    row = lax.broadcasted_iota(jnp.int32, (rows, rows), 0)
    col = lax.broadcasted_iota(jnp.int32, (rows, rows), 1)
    raw = s[:, W:]
    first = jnp.where(col > row, s[:, :rows], -jnp.inf)
    last = jnp.where(col <= row, raw, -jnp.inf)
    s = jnp.concatenate([first, s[:, rows:W], last], axis=1)
    top = jnp.max(s, axis=-1, keepdims=True)
    p = jnp.exp2((s - top) * score_scale).astype(BF16)
    soft = dot_nn(p, vbuf[pl.ds(b, W + rows), cols])
    v_own = vbuf[pl.ds(b + W, rows), cols]
    upper, lower = hi_lo(jnp.where(col <= row, raw, 0.0))
    return normalize(soft), dot_nn(upper, v_own) + dot_nn(lower, v_own)


def mix_block(q_ref, states, prior, soft, lin, b, block, h, rows):
    q = q_ref[pl.ds(b, rows), h * HD : (h + 1) * HD]
    s_upper, s_lower = hi_lo(states[block, h] + prior[h])
    lin += dot_nn(jnp.concatenate([q, q], axis=1), jnp.concatenate([s_upper, s_lower], axis=0))
    return (0.5 * (soft + normalize(lin))).astype(BF16)


def layer_kernel(
    rows, shards, groups,
    q_ref, k_hbm, v_hbm, w_hbm, out_ref,
    kbuf, vbuf, states, prior, totals, arrived, soft_keep, lin_keep, mixed, regrouped, w_all,
    local_sem, state_send, state_recv, rim_send, rim_recv, w_send, w_recv, mix_send, mix_recv,
):
    tok_rows, width = q_ref.shape
    heads_here = width // HD
    blocks = tok_rows // rows
    rim_blocks = W // rows
    own_rows = tok_rows // groups
    subs = own_rows // rows
    w_rows = w_hbm.shape[0]
    rounds = shards.bit_length() - 1
    me = lax.axis_index("seq")
    group = lax.axis_index("head")

    local = [
        pltpu.make_async_copy(k_hbm, kbuf.at[pl.ds(W, tok_rows)], local_sem.at[0]),
        pltpu.make_async_copy(v_hbm, vbuf.at[pl.ds(W, tok_rows)], local_sem.at[1]),
        pltpu.make_async_copy(w_hbm, w_all.at[pl.ds(me * w_rows, w_rows)], local_sem.at[2]),
    ]
    for c in local:
        c.start()

    barrier = pltpu.get_barrier_semaphore()
    for step in range(1, groups):
        peer = lax.rem(group + step, groups)
        pl.semaphore_signal(barrier, inc=1, device_id={"head": peer}, device_id_type=MESH)
    for r in range(rounds):
        pl.semaphore_signal(barrier, inc=1, device_id={"seq": flip(me, 1 << r)}, device_id_type=MESH)
    for step in (1, shards - 1):
        pl.semaphore_signal(
            barrier, inc=1, device_id={"seq": lax.rem(me + step, shards)}, device_id_type=MESH
        )
    pl.semaphore_wait(barrier, groups - 1 + rounds + 2)

    def rim_copies(n):
        out = []
        for which, (hbm, buf) in enumerate(((k_hbm, kbuf), (v_hbm, vbuf))):
            out.append(
                pltpu.make_async_remote_copy(
                    src_ref=hbm.at[pl.ds(tok_rows - W + n * rows, rows)],
                    dst_ref=buf.at[pl.ds(n * rows, rows)],
                    send_sem=rim_send.at[which, n],
                    recv_sem=rim_recv.at[which, n],
                    device_id={"seq": lax.rem(me + 1, shards)},
                    device_id_type=MESH,
                )
            )
        return out

    @pl.when(me < shards - 1)
    def _():
        for n in reversed(range(rim_blocks)):
            for c in rim_copies(n):
                c.start()

    for c in local:
        c.wait()

    @pl.when(me == 0)
    def _():
        kbuf[0:W] = jnp.broadcast_to(kbuf[W : W + 1], (W, width))
        vbuf[0:W] = jnp.zeros((W, width), BF16)

    for h in range(heads_here):
        cols = slice(h * HD, (h + 1) * HD)
        total = jnp.zeros((HD, HD), F32)
        for block in range(blocks):
            states[block, h] = total
            span = slice(W + block * rows, W + (block + 1) * rows)
            total += dot_tn(kbuf[span, cols], vbuf[span, cols])
        totals[0, h] = total
    prior[...] = jnp.zeros_like(prior)

    def state_copy(r, bit):
        return pltpu.make_async_remote_copy(
            src_ref=totals.at[r],
            dst_ref=arrived.at[r],
            send_sem=state_send.at[r],
            recv_sem=state_recv.at[r],
            device_id={"seq": flip(me, bit)},
            device_id_type=MESH,
        )

    state_copy(0, 1).start()

    def block_at(i):
        plain = jnp.where(i < blocks - rim_blocks, rim_blocks + i, blocks - 1 - i)
        if blocks != 2 * rim_blocks:
            return plain
        half = lax.div(i, 2)
        spread = jnp.where(lax.rem(i, 2) == 0, rim_blocks + half, rim_blocks - 1 - half)
        return jnp.where(2 * group >= groups, spread, plain)

    def await_rim(block):
        @pl.when((block < rim_blocks) & (me > 0))
        def _():
            for c in rim_copies(lax.rem(block, rim_blocks)):
                c.wait_recv()

    def mix_copy(block, source, target):
        sub = lax.rem(block, subs)
        return pltpu.make_async_remote_copy(
            src_ref=mixed.at[pl.ds(block * rows, rows)],
            dst_ref=regrouped.at[pl.ds(sub * rows, rows), pl.ds(source * width, width)],
            send_sem=mix_send.at[block],
            recv_sem=mix_recv.at[source, sub],
            device_id={"head": target},
            device_id_type=MESH,
        )

    def hand_on(block):
        target = lax.div(block, subs)

        @pl.when(target != group)
        def _():
            mix_copy(block, group, target).start()

        @pl.when(target == group)
        def _():
            c = pltpu.make_async_copy(
                mixed.at[pl.ds(block * rows, rows)],
                regrouped.at[pl.ds(lax.rem(block, subs) * rows, rows), pl.ds(group * width, width)],
                local_sem.at[0],
            )
            c.start()
            c.wait()

    def early(i, bit):
        block = block_at(i)
        b = pl.multiple_of(block * rows, rows)
        await_rim(block)
        for h in range(heads_here):
            soft_keep[i, h], lin_keep[i, h] = raw_block(q_ref, kbuf, vbuf, b, h, rows)
        state_copy(i, bit).wait()
        later = lax.rem(lax.div(me, bit), 2).astype(F32)
        prior[...] += arrived[i] * later
        totals[i + 1] = totals[i] + arrived[i]

        @pl.when(i + 1 < rounds)
        def _():
            state_copy(i + 1, 2 * bit).start()

        return 2 * bit

    lax.fori_loop(0, rounds, early, jnp.int32(1))

    spread_bits = [1 << r for r in range(1, rounds)]
    have = [me]
    counter = [0]
    pending = []

    def w_copy(block, bit):
        n = counter[0]
        counter[0] += 1
        place = pl.ds(pl.multiple_of(block * w_rows, w_rows), w_rows)
        c = pltpu.make_async_remote_copy(
            src_ref=w_all.at[place],
            dst_ref=w_all.at[place],
            send_sem=w_send.at[n],
            recv_sem=w_recv.at[n],
            device_id={"seq": flip(me, bit)},
            device_id_type=MESH,
        )
        c.start()
        return c

    def w_round(r):
        if r > 0:
            for c in waiting:
                c.wait()
            waiting.clear()
        fresh = have[len(have) // 2 :] if r > 0 else have
        if r < len(spread_bits):
            bit = jnp.where(lax.rem(me, 2) == 0, spread_bits[r], spread_bits[len(spread_bits) - 1 - r])
            waiting.extend(w_copy(block, bit) for block in have)
        pending.extend(w_copy(block, 1) for block in fresh)
        if r < len(spread_bits):
            have.extend([flip(block, bit) for block in have])

    waiting = []
    w_round(0)

    def late_mix(i, carry):
        block = block_at(i)
        b = pl.multiple_of(block * rows, rows)
        for h in range(heads_here):
            mixed[pl.ds(b, rows), h * HD : (h + 1) * HD] = mix_block(
                q_ref, states, prior, soft_keep[i, h], lin_keep[i, h], b, block, h, rows
            )
        hand_on(block)
        return carry

    lax.fori_loop(0, rounds, late_mix, 0)

    def one_block(i, carry):
        block = block_at(i)
        b = pl.multiple_of(block * rows, rows)
        await_rim(block)
        for h in range(heads_here):
            soft, lin = raw_block(q_ref, kbuf, vbuf, b, h, rows)
            mixed[pl.ds(b, rows), h * HD : (h + 1) * HD] = mix_block(
                q_ref, states, prior, soft, lin, b, block, h, rows
            )
        hand_on(block)
        return carry

    middle = min(rounds + 2, blocks)
    lax.fori_loop(rounds, middle, one_block, 0)
    w_round(1)
    lax.fori_loop(middle, blocks, one_block, 0)
    for r in range(2, len(spread_bits) + 1):
        w_round(r)

    for c in pending:
        c.wait()
    for step in range(1, groups):
        source = lax.rem(group + step, groups)
        for sub in range(subs):
            mix_copy(sub, source, source).wait_recv()

    tile = 256

    def project(n, carry):
        cols = pl.ds(pl.multiple_of(n * tile, tile), tile)
        out_ref[:, cols] = dot_nn(regrouped[...], w_all[:, cols]).astype(BF16)
        return carry

    lax.fori_loop(0, out_ref.shape[1] // tile, project, 0)

    def sent(block, carry):
        target = lax.div(block, subs)

        @pl.when(target != group)
        def _():
            mix_copy(block, group, target).wait_send()

        return carry

    lax.fori_loop(0, blocks, sent, 0)

    @pl.when(me < shards - 1)
    def _():
        for n in range(rim_blocks):
            for c in rim_copies(n):
                c.wait_send()


def on_device(queries, key_vectors, value_vectors, w_out):
    tok_rows, width = queries.shape
    heads_here = width // HD
    shards = lax.axis_size("seq")
    groups = lax.axis_size("head")
    own_rows = tok_rows // groups
    rows = min(256, own_rows)
    w_rows, model = w_out.shape
    rounds = shards.bit_length() - 1
    vmem = pl.BlockSpec(memory_space=pltpu.VMEM)
    hbm = pl.BlockSpec(memory_space=pl.ANY)
    dma = pltpu.SemaphoreType.DMA
    return pl.pallas_call(
        functools.partial(layer_kernel, rows, shards, groups),
        out_shape=jax.ShapeDtypeStruct((own_rows, model), BF16),
        in_specs=[vmem, hbm, hbm, hbm],
        out_specs=vmem,
        scratch_shapes=[
            pltpu.VMEM((W + tok_rows, width), BF16),
            pltpu.VMEM((W + tok_rows, width), BF16),
            pltpu.VMEM((tok_rows // rows, heads_here, HD, HD), F32),
            pltpu.VMEM((heads_here, HD, HD), F32),
            pltpu.VMEM((rounds + 1, heads_here, HD, HD), F32),
            pltpu.VMEM((rounds, heads_here, HD, HD), F32),
            pltpu.VMEM((rounds, heads_here, rows, HD), F32),
            pltpu.VMEM((rounds, heads_here, rows, HD), F32),
            pltpu.VMEM((tok_rows, width), BF16),
            pltpu.VMEM((own_rows, groups * width), BF16),
            pltpu.VMEM((shards * w_rows, model), BF16),
            dma((3,)),
            dma((rounds,)),
            dma((rounds,)),
            dma((2, W // rows)),
            dma((2, W // rows)),
            dma((shards - 1,)),
            dma((shards - 1,)),
            dma((tok_rows // rows,)),
            dma((groups, own_rows // rows)),
        ],
        compiler_params=pltpu.CompilerParams(
            collective_id=0, has_side_effects=True, vmem_limit_bytes=56 << 20
        ),
        cost_estimate=pl.CostEstimate(
            flops=2 * tok_rows * 2800 * width + 2 * own_rows * model * model,
            bytes_accessed=16 << 20,
            transcendentals=0,
        ),
    )(queries, key_vectors, value_vectors, w_out)


def solution(mesh):
    placed = (P("seq", "head"), P("seq", "head"), P("seq", "head"), P("seq", None))
    return jax.shard_map(
        on_device, mesh=mesh, in_specs=placed, out_specs=P(("seq", "head"), None), check_vma=False
    )
```

```python
import functools
import math

import jax
import jax.numpy as jnp
from jax import lax
from jax.experimental import pallas as pl
from jax.experimental.pallas import tpu as pltpu
from jax.sharding import PartitionSpec as P

HD = 128
W = 1024
NORM_EPS = 1e-06
F32 = jnp.float32
BF16 = jnp.bfloat16
MESH = pl.DeviceIdType.MESH


def dot_nt(a, b):
    return lax.dot_general(a, b, (((1,), (1,)), ((), ())), preferred_element_type=F32)


def dot_tn(a, b):
    return lax.dot_general(a, b, (((0,), (0,)), ((), ())), preferred_element_type=F32)


def dot_nn(a, b):
    return jnp.dot(a, b, preferred_element_type=F32)


def normalize(branch):
    return branch * lax.rsqrt(jnp.mean(branch * branch, axis=-1, keepdims=True) + NORM_EPS)


def hi_lo(values):
    upper = values.astype(BF16)
    lower = (values - upper.astype(F32)).astype(BF16)
    return upper, lower


def flip(index, bit):
    return index + bit - 2 * bit * lax.rem(lax.div(index, bit), 2)


def raw_block(q_ref, kbuf, vbuf, b, h, rows):
    cols = slice(h * HD, (h + 1) * HD)
    score_scale = math.log2(math.e) / math.sqrt(HD)
    q = q_ref[pl.ds(b, rows), cols]
    s = dot_nt(q, kbuf[pl.ds(b, W + rows), cols])
    row = lax.broadcasted_iota(jnp.int32, (rows, rows), 0)
    col = lax.broadcasted_iota(jnp.int32, (rows, rows), 1)
    raw = s[:, W:]
    first = jnp.where(col > row, s[:, :rows], -jnp.inf)
    last = jnp.where(col <= row, raw, -jnp.inf)
    s = jnp.concatenate([first, s[:, rows:W], last], axis=1)
    top = jnp.max(s, axis=-1, keepdims=True)
    p = jnp.exp2((s - top) * score_scale).astype(BF16)
    soft = dot_nn(p, vbuf[pl.ds(b, W + rows), cols])
    v_own = vbuf[pl.ds(b + W, rows), cols]
    upper, lower = hi_lo(jnp.where(col <= row, raw, 0.0))
    return normalize(soft), dot_nn(upper, v_own) + dot_nn(lower, v_own)


def mix_block(q_ref, states, prior, soft, lin, b, block, h, rows):
    q = q_ref[pl.ds(b, rows), h * HD : (h + 1) * HD]
    s_upper, s_lower = hi_lo(states[block, h] + prior[h])
    lin += dot_nn(jnp.concatenate([q, q], axis=1), jnp.concatenate([s_upper, s_lower], axis=0))
    return (0.5 * (soft + normalize(lin))).astype(BF16)


def layer_kernel(
    rows, shards, groups,
    q_ref, k_hbm, v_hbm, w_hbm, out_ref,
    kbuf, vbuf, states, prior, totals, arrived, soft_keep, lin_keep, mixed, regrouped, w_all, sums,
    local_sem, state_send, state_recv, rim_send, rim_recv, w_send, w_recv, mix_send, mix_recv,
):
    tok_rows, width = q_ref.shape
    heads_here = width // HD
    blocks = tok_rows // rows
    rim_blocks = W // rows
    own_rows = tok_rows // groups
    subs = own_rows // rows
    w_rows = w_hbm.shape[0]
    rounds = shards.bit_length() - 1
    me = lax.axis_index("seq")
    group = lax.axis_index("head")

    local = [
        pltpu.make_async_copy(k_hbm, kbuf.at[pl.ds(W, tok_rows)], local_sem.at[0]),
        pltpu.make_async_copy(v_hbm, vbuf.at[pl.ds(W, tok_rows)], local_sem.at[1]),
        pltpu.make_async_copy(w_hbm, w_all.at[pl.ds(me * w_rows, w_rows)], local_sem.at[2]),
    ]
    for c in local:
        c.start()

    barrier = pltpu.get_barrier_semaphore()
    for step in range(1, groups):
        peer = lax.rem(group + step, groups)
        pl.semaphore_signal(barrier, inc=1, device_id={"head": peer}, device_id_type=MESH)
    for r in range(rounds):
        pl.semaphore_signal(barrier, inc=1, device_id={"seq": flip(me, 1 << r)}, device_id_type=MESH)
    for step in (1, shards - 1):
        pl.semaphore_signal(
            barrier, inc=1, device_id={"seq": lax.rem(me + step, shards)}, device_id_type=MESH
        )
    pl.semaphore_wait(barrier, groups - 1 + rounds + 2)

    def rim_copies(n):
        out = []
        for which, (hbm, buf) in enumerate(((k_hbm, kbuf), (v_hbm, vbuf))):
            out.append(
                pltpu.make_async_remote_copy(
                    src_ref=hbm.at[pl.ds(tok_rows - W + n * rows, rows)],
                    dst_ref=buf.at[pl.ds(n * rows, rows)],
                    send_sem=rim_send.at[which, n],
                    recv_sem=rim_recv.at[which, n],
                    device_id={"seq": lax.rem(me + 1, shards)},
                    device_id_type=MESH,
                )
            )
        return out

    local[2].wait()
    spread_bits = [1 << r for r in range(1, rounds)]
    have = [me]
    counter = [0]
    pending = []

    def w_copy(block, bit):
        n = counter[0]
        counter[0] += 1
        place = pl.ds(pl.multiple_of(block * w_rows, w_rows), w_rows)
        c = pltpu.make_async_remote_copy(
            src_ref=w_all.at[place],
            dst_ref=w_all.at[place],
            send_sem=w_send.at[n],
            recv_sem=w_recv.at[n],
            device_id={"seq": flip(me, bit)},
            device_id_type=MESH,
        )
        c.start()
        return c

    def w_round(r):
        if r > 0:
            for c in waiting:
                c.wait()
            waiting.clear()
        fresh = have[len(have) // 2 :] if r > 0 else have
        if r < len(spread_bits):
            bit = jnp.where(lax.rem(me, 2) == 0, spread_bits[r], spread_bits[len(spread_bits) - 1 - r])
            waiting.extend(w_copy(block, bit) for block in have)
        pending.extend(w_copy(block, 1) for block in fresh)
        if r < len(spread_bits):
            have.extend([flip(block, bit) for block in have])

    waiting = []
    w_round(0)
    for c in local[:2]:
        c.wait()

    @pl.when(me == 0)
    def _():
        kbuf[0:W] = jnp.broadcast_to(kbuf[W : W + 1], (W, width))
        vbuf[0:W] = jnp.zeros((W, width), BF16)

    for h in range(heads_here):
        cols = slice(h * HD, (h + 1) * HD)
        total = jnp.zeros((HD, HD), F32)
        for block in range(blocks):
            states[block, h] = total
            span = slice(W + block * rows, W + (block + 1) * rows)
            total += dot_tn(kbuf[span, cols], vbuf[span, cols])
        totals[0, h] = total
    prior[...] = jnp.zeros_like(prior)

    def state_copy(r, bit):
        return pltpu.make_async_remote_copy(
            src_ref=totals.at[r],
            dst_ref=arrived.at[r],
            send_sem=state_send.at[r],
            recv_sem=state_recv.at[r],
            device_id={"seq": flip(me, bit)},
            device_id_type=MESH,
        )

    state_copy(0, 1).start()

    inner = list(range(rim_blocks, blocks))
    outer = list(reversed(range(rim_blocks)))
    plain = inner + outer
    spread, inner = inner[:rounds], inner[rounds:]
    while inner or outer:
        spread += outer[:2] + inner[:1]
        inner, outer = inner[1:], outer[2:]

    def block_at(i):
        block = 0
        for j in range(blocks):
            chosen = jnp.where(2 * group >= groups, spread[j], plain[j])
            block = block + jnp.where(i == j, chosen, 0)
        return block

    def await_rim(block):
        @pl.when((block < rim_blocks) & (me > 0))
        def _():
            for c in rim_copies(lax.rem(block, rim_blocks)):
                c.wait_recv()

    def mix_copy(block, source, target):
        sub = lax.rem(block, subs)
        return pltpu.make_async_remote_copy(
            src_ref=mixed.at[pl.ds(block * rows, rows)],
            dst_ref=regrouped.at[pl.ds(sub * rows, rows), pl.ds(source * width, width)],
            send_sem=mix_send.at[block],
            recv_sem=mix_recv.at[source, sub],
            device_id={"head": target},
            device_id_type=MESH,
        )

    def hand_on(block):
        target = lax.div(block, subs)

        @pl.when(target != group)
        def _():
            mix_copy(block, group, target).start()

        @pl.when(target == group)
        def _():
            c = pltpu.make_async_copy(
                mixed.at[pl.ds(block * rows, rows)],
                regrouped.at[pl.ds(lax.rem(block, subs) * rows, rows), pl.ds(group * width, width)],
                local_sem.at[0],
            )
            c.start()
            c.wait()

    def early(i, bit):
        block = block_at(i)
        b = pl.multiple_of(block * rows, rows)
        await_rim(block)
        for h in range(heads_here):
            soft_keep[i, h], lin_keep[i, h] = raw_block(q_ref, kbuf, vbuf, b, h, rows)
        state_copy(i, bit).wait()
        later = lax.rem(lax.div(me, bit), 2).astype(F32)
        prior[...] += arrived[i] * later
        totals[i + 1] = totals[i] + arrived[i]

        @pl.when(i + 1 < rounds)
        def _():
            state_copy(i + 1, 2 * bit).start()

        @pl.when((i == 0) & (me < shards - 1))
        def _():
            for n in reversed(range(rim_blocks)):
                for c in rim_copies(n):
                    c.start()

        return 2 * bit

    lax.fori_loop(0, rounds, early, jnp.int32(1))

    w_round(1)

    def late_mix(i, carry):
        block = block_at(i)
        b = pl.multiple_of(block * rows, rows)
        for h in range(heads_here):
            mixed[pl.ds(b, rows), h * HD : (h + 1) * HD] = mix_block(
                q_ref, states, prior, soft_keep[i, h], lin_keep[i, h], b, block, h, rows
            )
        hand_on(block)
        return carry

    lax.fori_loop(0, rounds, late_mix, 0)

    def one_block(i, carry):
        block = block_at(i)
        b = pl.multiple_of(block * rows, rows)
        await_rim(block)
        for h in range(heads_here):
            soft, lin = raw_block(q_ref, kbuf, vbuf, b, h, rows)
            mixed[pl.ds(b, rows), h * HD : (h + 1) * HD] = mix_block(
                q_ref, states, prior, soft, lin, b, block, h, rows
            )
        hand_on(block)
        return carry

    lax.fori_loop(rounds, blocks, one_block, 0)
    for r in range(2, len(spread_bits) + 1):
        w_round(r)

    for c in pending:
        c.wait()
    tile = 256
    for m in range(groups):
        source = group
        for r in range(groups.bit_length() - 1):
            if m >> r & 1:
                source = flip(source, 1 << r)
        if m > 0:
            for sub in range(subs):
                mix_copy(sub, source, source).wait_recv()
        held = pl.ds(pl.multiple_of(source * width, width), width)

        def project(n, carry):
            cols = pl.ds(pl.multiple_of(n * tile, tile), tile)
            part = dot_nn(regrouped[:, held], w_all[held, cols])
            if m > 0:
                part += sums[:, cols]
            if m < groups - 1:
                sums[:, cols] = part
            else:
                out_ref[:, cols] = part.astype(BF16)
            return carry

        lax.fori_loop(0, out_ref.shape[1] // tile, project, 0)

    def sent(block, carry):
        target = lax.div(block, subs)

        @pl.when(target != group)
        def _():
            mix_copy(block, group, target).wait_send()

        return carry

    lax.fori_loop(0, blocks, sent, 0)

    @pl.when(me < shards - 1)
    def _():
        for n in range(rim_blocks):
            for c in rim_copies(n):
                c.wait_send()


def on_device(queries, key_vectors, value_vectors, w_out):
    tok_rows, width = queries.shape
    heads_here = width // HD
    shards = lax.axis_size("seq")
    groups = lax.axis_size("head")
    own_rows = tok_rows // groups
    rows = min(256, own_rows)
    w_rows, model = w_out.shape
    rounds = shards.bit_length() - 1
    vmem = pl.BlockSpec(memory_space=pltpu.VMEM)
    hbm = pl.BlockSpec(memory_space=pl.ANY)
    dma = pltpu.SemaphoreType.DMA
    return pl.pallas_call(
        functools.partial(layer_kernel, rows, shards, groups),
        out_shape=jax.ShapeDtypeStruct((own_rows, model), BF16),
        in_specs=[vmem, hbm, hbm, hbm],
        out_specs=vmem,
        scratch_shapes=[
            pltpu.VMEM((W + tok_rows, width), BF16),
            pltpu.VMEM((W + tok_rows, width), BF16),
            pltpu.VMEM((tok_rows // rows, heads_here, HD, HD), F32),
            pltpu.VMEM((heads_here, HD, HD), F32),
            pltpu.VMEM((rounds + 1, heads_here, HD, HD), F32),
            pltpu.VMEM((rounds, heads_here, HD, HD), F32),
            pltpu.VMEM((rounds, heads_here, rows, HD), F32),
            pltpu.VMEM((rounds, heads_here, rows, HD), F32),
            pltpu.VMEM((tok_rows, width), BF16),
            pltpu.VMEM((own_rows, groups * width), BF16),
            pltpu.VMEM((shards * w_rows, model), BF16),
            pltpu.VMEM((own_rows, model), F32),
            dma((3,)),
            dma((rounds,)),
            dma((rounds,)),
            dma((2, W // rows)),
            dma((2, W // rows)),
            dma((shards - 1,)),
            dma((shards - 1,)),
            dma((tok_rows // rows,)),
            dma((groups, own_rows // rows)),
        ],
        compiler_params=pltpu.CompilerParams(
            collective_id=0, has_side_effects=True, vmem_limit_bytes=56 << 20
        ),
        cost_estimate=pl.CostEstimate(
            flops=2 * tok_rows * 2800 * width + 2 * own_rows * model * model,
            bytes_accessed=16 << 20,
            transcendentals=0,
        ),
    )(queries, key_vectors, value_vectors, w_out)


def solution(mesh):
    placed = (P("seq", "head"), P("seq", "head"), P("seq", "head"), P("seq", None))
    return jax.shard_map(
        on_device, mesh=mesh, in_specs=placed, out_specs=P(("seq", "head"), None), check_vma=False
    )
```
